32 devices in a mesh: ctx: 4 (over z), exp: 2 (over x), tp: 4 (over y, core).
Axes of the slice: x: 2, y: 2, z: 4, core: 2. Of those that a mesh axis runs over, the one named last changes fastest.
Arguments:
- queries: bfloat16 [4096, 4096], P(('ctx', 'exp'), 'tp'), may hold values from -6 to 6
- key_vectors: bfloat16 [4096, 4096], P(('ctx', 'exp'), 'tp'), may hold values from -6 to 6
- value_vectors: bfloat16 [4096, 4096], P(('ctx', 'exp'), 'tp'), may hold values from -6 to 6
- decay_rate: float32 [32], P('tp'), may hold values from 1e-07 to 0.05
- norm_gain: float32 [4096], P('tp'), may hold values from 0.5 to 1.5
Outputs:
- normed: bfloat16 [4096, 4096], P(('ctx', 'exp'), 'tp')
The draws below stay inside these ranges and needn't reach their ends.
All inputs are finite; a program needn't handle non-finite values.
Results may differ from the reference program's by a relative error of at most 0.0052.
Values sent between devices are 32-bit elements; how exact they have to be, the bound alone decides.
No kernel may reach another device: no remote copies, remote signals or barrier semaphores. Data moves between devices by JAX's collectives and lax.ppermute only.
A program may use at most 128 MiB of HBM per device.

```python
import math
import jax
import jax.numpy as jnp
from jax import lax

HEADS = 32
HEAD_DIM = 128
BLK = 256
SEQ = 4096


def steps_of(key, shape, cuts, smallest, high):
    def one(axis_at, parts):
        heights = jax.random.uniform(jax.random.fold_in(jax.random.fold_in(key, 6), axis_at), (parts,), jnp.float32, smallest / len(cuts), high / len(cuts))
        return jnp.repeat(jnp.exp(heights), shape[axis_at] // parts).reshape((-1,) + (1,) * (len(shape) - axis_at - 1))

    level = one(*cuts[0])
    for cut in cuts[1:]:
        level = level * one(*cut)
    return level


def normal_values(rng, extent, scale, limit, split=(), held_as=jnp.bfloat16):
    loudness = steps_of(rng, extent, split, -0.22, 0.18) if split else 1.0
    entries = jax.random.normal(rng, extent, jnp.float32) * scale * loudness
    return jnp.minimum(jnp.maximum(entries, -limit), limit).astype(held_as)


def setup_inputs(seed: int = 0) -> dict:
    arg_keys = jax.random.split(jax.random.key(seed), 6)
    return {
        "queries": normal_values(arg_keys[0], (SEQ, HEADS * HEAD_DIM), 1.0, 6.0, ((0, 8), (1, 4))),
        "key_vectors": normal_values(arg_keys[1], (SEQ, HEADS * HEAD_DIM), 1.0, 6.0, ((0, 8), (1, 4))),
        "value_vectors": normal_values(arg_keys[2], (SEQ, HEADS * HEAD_DIM), 1.0, 6.0, ((0, 8), (1, 4))),
        "decay_rate": jnp.clip(jnp.exp(math.log(0.05) - 13.122363 * jax.random.uniform(arg_keys[3], (HEADS,), jnp.float32) ** steps_of(arg_keys[3], (HEADS,), ((0, 4),), -0.2, 0.2)), 1.0000000116860974e-07, 0.05),
        "norm_gain": jnp.clip(1.0 + 0.1 * jax.random.normal(arg_keys[4], (HEADS * HEAD_DIM,), jnp.float32), 0.5, 1.5),
    }


def reference(queries, key_vectors, value_vectors, decay_rate, norm_gain):
    seq_len = queries.shape[0]
    blocks = seq_len // BLK
    query_blocks = queries.reshape(blocks, BLK, HEADS, HEAD_DIM)
    key_blocks = key_vectors.reshape(blocks, BLK, HEADS, HEAD_DIM)
    value_blocks = value_vectors.reshape(blocks, BLK, HEADS, HEAD_DIM)
    offsets = jnp.arange(BLK, dtype=jnp.float32)
    spread = offsets[:, None] - offsets[None, :]
    causal = spread >= 0
    rates = decay_rate[:, None, None]
    weight = jnp.where(causal[None], jnp.exp(-rates * jnp.maximum(spread, 0.0)[None]), 0.0)
    inner_decay = jnp.exp(-decay_rate[None, :] * offsets[:, None])
    tail_decay = jnp.exp(-decay_rate[None, :] * (BLK - offsets)[:, None])
    block_decay = jnp.exp(-decay_rate * BLK)[:, None, None]

    def advance(carry_state, block_data):
        query_block, key_block, value_block = block_data
        query_wide = query_block.astype(jnp.float32)
        value_wide = value_block.astype(jnp.float32)
        scores = jnp.einsum('thd,shd->hts', query_wide, key_block.astype(jnp.float32))
        mixing = (scores * weight).astype(jnp.bfloat16)
        local_part = jnp.einsum('hts,she->the', mixing.astype(jnp.float32), value_wide)
        state_low = lax.optimization_barrier(carry_state.astype(jnp.bfloat16))
        carried = jnp.einsum('thd,hde->the', query_wide, state_low.astype(jnp.float32)) * inner_decay[:, :, None]
        scaled_keys = (key_block.astype(jnp.float32) * tail_decay[:, :, None]).astype(jnp.bfloat16)
        block_term = jnp.einsum('shd,she->hde', scaled_keys.astype(jnp.float32), value_wide)
        return (block_decay * carry_state + block_term, local_part + carried)
    start_state = jnp.zeros((HEADS, HEAD_DIM, HEAD_DIM), jnp.float32)
    unused, attended = lax.scan(advance, start_state, (query_blocks, key_blocks, value_blocks))
    attended = attended.reshape(seq_len, HEADS * HEAD_DIM)
    mean_square = lax.optimization_barrier(jnp.mean(attended * attended, axis=1, keepdims=True))
    normed = attended * lax.rsqrt(mean_square + 1e-06) * norm_gain[None, :]
    return normed.astype(jnp.bfloat16)
```

```python
import functools
import jax
import jax.numpy as jnp
from jax import lax
from jax.experimental import pallas as pl
from jax.experimental.pallas import tpu as pltpu
from jax.sharding import PartitionSpec as P

HEAD_DIM = 128
BLK = 256
F32 = jnp.float32
BF16 = jnp.bfloat16


def dot(a, b, dims, precision=None):
    return lax.dot_general(a, b, (dims, ((), ())), precision=precision, preferred_element_type=F32)


def params(mib=32):
    return pltpu.CompilerParams(vmem_limit_bytes=mib << 20)


def spread_kernel(who, rate_ref, key_ref, value_ref, *outs, group, blocks, heads):
    states, terms = outs[:group], outs[group]
    d = pl.program_id(0)
    first = (who[0] ^ d) * heads
    left = (BLK - lax.broadcasted_iota(jnp.int32, (BLK, HEAD_DIM), 0)).astype(F32)
    results = []
    for h in range(heads):
        rate = rate_ref[first + h]
        cols = slice(h * HEAD_DIM, (h + 1) * HEAD_DIM)
        tail = jnp.exp(-rate * left)
        block_decay = jnp.exp(jnp.full((HEAD_DIM, HEAD_DIM), -rate * BLK, F32))
        own = None
        for b in range(blocks):
            rows = slice(b * BLK, (b + 1) * BLK)
            keys = (key_ref[rows, cols].astype(F32) * tail).astype(BF16)
            term = dot(keys, value_ref[rows, cols], ((0,), (0,)))
            if b < blocks - 1:
                terms[b, 0, cols, :] = term
            own = term if own is None else block_decay * own + term
        results.append(own)
    for i in range(group):
        @pl.when(d == i)
        def _():
            for h in range(heads):
                states[i][h * HEAD_DIM : (h + 1) * HEAD_DIM, :] = results[h]


def local_kernel(rate_ref, query_ref, key_ref, value_ref, out_ref, *, blocks):
    rate = rate_ref[pl.program_id(0)]
    t = lax.broadcasted_iota(jnp.int32, (BLK, BLK), 0)
    s = lax.broadcasted_iota(jnp.int32, (BLK, BLK), 1)
    apart = (t - s).astype(F32)
    weight = jnp.where(apart >= 0, jnp.exp(-rate * jnp.maximum(apart, 0.0)), 0.0)
    for b in range(blocks):
        rows = slice(b * BLK, (b + 1) * BLK)
        scores = dot(query_ref[rows, :], key_ref[rows, :], ((1,), (1,)))
        mixing = (scores * weight).astype(BF16)
        out_ref[rows, :] = dot(mixing, value_ref[rows, :], ((1,), (0,)))


def span_weight(rate, gap, span):
    wide = jnp.full((8, HEAD_DIM), jnp.maximum(gap, 0).astype(F32) * span, F32)
    return jnp.where(gap >= 0, jnp.exp(-rate * wide), 0.0)[:1, :]


def total_kernel(who, rate_ref, *refs, group, heads, span):
    slots, out = refs[:group], refs[group]
    me = who[0]
    for h in range(heads):
        rate = rate_ref[me * heads + h]
        rows = slice(h * HEAD_DIM, (h + 1) * HEAD_DIM)
        total = None
        for e in range(group):
            part = span_weight(rate, group - 1 - (me ^ e), span) * slots[e][rows, :]
            total = part if total is None else total + part
        out[rows, :] = total


def carry_kernel(who, rate_ref, before_ref, *refs, group, heads, span):
    slots, outs = refs[:group], refs[group:]
    me = who[0]
    for h in range(heads):
        rate = rate_ref[me * heads + h]
        rows = slice(h * HEAD_DIM, (h + 1) * HEAD_DIM)
        parts = [slots[e][rows, :] for e in range(group)]
        before = before_ref[rows, :]
        for d in range(group):
            carry = span_weight(rate, me ^ d, span) * before
            for e in range(group):
                if e != d:
                    carry = carry + span_weight(rate, (me ^ d) - (me ^ e) - 1, span) * parts[e]
            outs[d][rows, :] = carry


def carried_kernel(who, rate_ref, query_ref, local_ref, terms_ref, *refs, group, blocks, heads):
    carries, att_ref, squares_ref, acc_ref = refs[:group], refs[group], refs[group + 1], refs[group + 2]
    d = pl.program_id(0)
    first = (who[0] ^ d) * heads
    offset = lax.broadcasted_iota(jnp.int32, (BLK, HEAD_DIM), 0).astype(F32)

    @pl.when(d == 0)
    def _():
        acc_ref[...] = jnp.zeros_like(acc_ref)

    def work(carry_ref):
        for h in range(heads):
            rate = rate_ref[first + h]
            cols = slice(h * HEAD_DIM, (h + 1) * HEAD_DIM)
            inner = jnp.exp(-rate * offset)
            block_decay = jnp.exp(jnp.full((HEAD_DIM, HEAD_DIM), -rate * BLK, F32))
            state = carry_ref[cols, :]
            for b in range(blocks):
                rows = slice(b * BLK, (b + 1) * BLK)
                carried = dot(query_ref[rows, cols], state.astype(BF16), ((1,), (0,)))
                att = local_ref[rows, cols] + carried * inner
                att_ref[rows, cols] = att
                acc_ref[rows, :] += att * att
                if b < blocks - 1:
                    state = block_decay * state + terms_ref[b, 0, cols, :]

    for i in range(group):
        pl.when(d == i)(functools.partial(work, carries[i]))

    @pl.when(d == group - 1)
    def _():
        ones = jnp.ones((8, HEAD_DIM), F32)
        squares_ref[...] = dot(ones, acc_ref[...], ((1,), (1,)), lax.Precision.HIGHEST)


def norm_kernel(*refs, features, count):
    squares, gain_ref, att_ref, out_ref = refs[:count], refs[count], refs[count + 1], refs[count + 2]
    total = squares[0][...]
    for other in squares[1:]:
        total = total + other[...]
    inverse = lax.rsqrt(total / features + 1e-06)
    pick = (lax.broadcasted_iota(jnp.int32, (8, HEAD_DIM), 0) == 0).astype(F32)
    column = dot(inverse, pick, ((0,), (0,)), lax.Precision.HIGHEST)
    for c in range(att_ref.shape[1] // HEAD_DIM):
        cols = slice(c * HEAD_DIM, (c + 1) * HEAD_DIM)
        out_ref[:, cols] = (att_ref[:, cols] * column * gain_ref[:, cols]).astype(BF16)


def local(queries, key_vectors, value_vectors, decay_rate, norm_gain, *, zp, nc, ne, nt):
    rows, width = queries.shape
    heads_all = width // HEAD_DIM
    blocks = rows // BLK
    group = zp * ne
    heads = heads_all // group
    part = heads * HEAD_DIM
    z, x = lax.axis_index("ctx"), lax.axis_index("exp")
    who = jnp.reshape((z % zp) * ne + x, (1,)).astype(jnp.int32)
    smem = pl.BlockSpec(memory_space=pltpu.SMEM)
    vmem = pl.BlockSpec(memory_space=pltpu.VMEM)
    whole_state = pl.BlockSpec((part, HEAD_DIM), lambda d, w: (0, 0))
    mine = pl.BlockSpec((rows, part), lambda d, w: (0, w[0] ^ d))
    term_block = pl.BlockSpec((blocks - 1, 1, part, HEAD_DIM), lambda d, w: (0, d, 0, 0))
    state_type = jax.ShapeDtypeStruct((part, HEAD_DIM), F32)

    *slots, terms = pl.pallas_call(
        functools.partial(spread_kernel, group=group, blocks=blocks, heads=heads),
        grid_spec=pltpu.PrefetchScalarGridSpec(
            num_scalar_prefetch=1, grid=(group,),
            in_specs=[smem, mine, mine],
            out_specs=[whole_state] * group + [term_block],
        ),
        out_shape=[state_type] * group + [jax.ShapeDtypeStruct((blocks - 1, group, part, HEAD_DIM), F32)],
        compiler_params=params(),
        name="spread",
    )(who, decay_rate, key_vectors, value_vectors)

    def swap(value, d):
        pairs = []
        for zz in range(nc):
            for xx in range(ne):
                m = ((zz % zp) * ne + xx) ^ d
                pairs.append((zz * ne + xx, (zz // zp * zp + m // ne) * ne + m % ne))
        return lax.ppermute(value, ("ctx", "exp"), pairs)

    order = list(range(group - 1, 0, -1))
    got = {d: swap(slots[d], d) for d in order}
    slots = [slots[0]] + [got[d] for d in range(1, group)]

    one_head = pl.BlockSpec((rows, HEAD_DIM), lambda h: (0, h))
    local_part = pl.pallas_call(
        functools.partial(local_kernel, blocks=blocks),
        grid=(heads_all,),
        in_specs=[smem, one_head, one_head, one_head],
        out_specs=one_head,
        out_shape=jax.ShapeDtypeStruct((rows, width), F32),
        compiler_params=params(),
        cost_estimate=pl.CostEstimate(flops=4 * rows * BLK * width, bytes_accessed=10 * rows * width, transcendentals=0),
        name="local_part",
    )(decay_rate, queries, key_vectors, value_vectors)

    span = float(rows)
    total = pl.pallas_call(
        functools.partial(total_kernel, group=group, heads=heads, span=span),
        in_specs=[smem, smem] + [vmem] * group,
        out_specs=vmem,
        out_shape=state_type,
        compiler_params=params(),
        name="group_total",
    )(who, decay_rate, *slots)
    groups = nc // zp
    before = lax.ppermute(total, "ctx", [(zz, zz + zp) for zz in range(nc - zp)])
    step = 1
    while step < groups - 1:
        rates = lax.dynamic_slice_in_dim(decay_rate, who[0] * heads, heads)
        scale = jnp.repeat(jnp.exp(-rates * (span * group * step)), HEAD_DIM)[:, None]
        moved = lax.ppermute(before, "ctx", [(zz, zz + zp * step) for zz in range(nc - zp * step)])
        before = before + scale * moved
        step *= 2

    carries = pl.pallas_call(
        functools.partial(carry_kernel, group=group, heads=heads, span=span),
        in_specs=[smem, smem] + [vmem] * (group + 1),
        out_specs=[vmem] * group,
        out_shape=[state_type] * group,
        compiler_params=params(),
        name="carry",
    )(who, decay_rate, before, *slots)
    got = {d: swap(carries[d], d) for d in order}
    carries = [carries[0]] + [got[d] for d in range(1, group)]

    attended, squares = pl.pallas_call(
        functools.partial(carried_kernel, group=group, blocks=blocks, heads=heads),
        grid_spec=pltpu.PrefetchScalarGridSpec(
            num_scalar_prefetch=1, grid=(group,),
            in_specs=[smem, mine, mine, term_block] + [whole_state] * group,
            out_specs=[mine, pl.BlockSpec((8, rows), lambda d, w: (0, 0))],
            scratch_shapes=[pltpu.VMEM((rows, HEAD_DIM), F32)],
        ),
        out_shape=[jax.ShapeDtypeStruct((rows, width), F32), jax.ShapeDtypeStruct((8, rows), F32)],
        compiler_params=params(),
        name="carried",
    )(who, decay_rate, queries, local_part, terms, *carries)

    if nt & (nt - 1) == 0:
        swaps = [[(i, i ^ d) for i in range(nt)] for d in range(1, nt)]
    else:
        swaps = [[(i, (i + d) % nt) for i in range(nt)] for d in range(1, nt)]
    sums = [squares] + [lax.ppermute(squares, "tp", pairs) for pairs in swaps[::-1]]

    return pl.pallas_call(
        functools.partial(norm_kernel, features=float(width * nt), count=nt),
        in_specs=[vmem] * (nt + 2),
        out_specs=vmem,
        out_shape=jax.ShapeDtypeStruct((rows, width), BF16),
        compiler_params=params(),
        name="norm",
    )(*sums, norm_gain[None, :], attended)


def solution(mesh):
    nc, ne, nt = mesh.shape["ctx"], mesh.shape["exp"], mesh.shape["tp"]

    def whole(queries, key_vectors, value_vectors, decay_rate, norm_gain):
        heads_local = decay_rate.shape[0] // nt
        zp = 2 if nc % 2 == 0 and heads_local % (2 * ne) == 0 else 1
        return jax.shard_map(
            functools.partial(local, zp=zp, nc=nc, ne=ne, nt=nt),
            mesh=mesh,
            in_specs=(P(("ctx", "exp"), "tp"),) * 3 + (P("tp"), P("tp")),
            out_specs=P(("ctx", "exp"), "tp"),
            check_vma=False,
        )(queries, key_vectors, value_vectors, decay_rate, norm_gain)

    return whole
```

```python
import functools
import jax
import jax.numpy as jnp
from jax import lax
from jax.experimental import pallas as pl
from jax.experimental.pallas import tpu as pltpu
from jax.sharding import PartitionSpec as P

HEAD_DIM = 128
BLK = 256
F32 = jnp.float32
BF16 = jnp.bfloat16


def dot(a, b, dims, precision=None):
    return lax.dot_general(a, b, (dims, ((), ())), precision=precision, preferred_element_type=F32)


def params(mib=32):
    return pltpu.CompilerParams(vmem_limit_bytes=mib << 20)


def spread_kernel(who, rate_hbm, key_hbm, value_hbm, *refs, group, blocks, heads, order):
    states, terms = refs[:group], refs[group]
    rate_ref, key_ref, value_ref, sems, rate_sem = refs[group + 1 :]
    part = heads * HEAD_DIM

    def copies(d):
        cols = pl.ds(pl.multiple_of((who[0] ^ d) * part, part), part)
        return (
            pltpu.make_async_copy(key_hbm.at[:, cols], key_ref.at[d], sems.at[0, d]),
            pltpu.make_async_copy(value_hbm.at[:, cols], value_ref.at[d], sems.at[1, d]),
        )

    rate_copy = pltpu.make_async_copy(rate_hbm, rate_ref, rate_sem)
    rate_copy.start()
    for d in order:
        for copy in copies(d):
            copy.start()
    left = (BLK - lax.broadcasted_iota(jnp.int32, (BLK, HEAD_DIM), 0)).astype(F32)
    rate_copy.wait()
    for d in order:
        rates = [rate_ref[(who[0] ^ d) * heads + h] for h in range(heads)]
        tails = [jnp.exp(-rate * left) for rate in rates]
        for copy in copies(d):
            copy.wait()
        for h in range(heads):
            cols = slice(h * HEAD_DIM, (h + 1) * HEAD_DIM)
            block_decay = jnp.exp(jnp.full((8, HEAD_DIM), -rates[h] * BLK, F32))[:1, :]
            own = None
            for b in range(blocks):
                rows = slice(b * BLK, (b + 1) * BLK)
                keys = (key_ref[d, rows, cols].astype(F32) * tails[h]).astype(BF16)
                term = dot(keys, value_ref[d, rows, cols], ((0,), (0,)))
                if b < blocks - 1:
                    terms[b, d, cols, :] = term
                own = term if own is None else block_decay * own + term
            states[d][cols, :] = own


def local_kernel(rate_ref, query_ref, key_ref, value_ref, out_ref, inner_ref, *, blocks):
    rate = rate_ref[pl.program_id(0)]
    t = lax.broadcasted_iota(jnp.int32, (BLK, BLK), 0)
    s = lax.broadcasted_iota(jnp.int32, (BLK, BLK), 1)
    apart = (t - s).astype(F32)
    weight = jnp.where(apart >= 0, jnp.exp(-rate * jnp.maximum(apart, 0.0)), 0.0)
    inner_ref[0] = jnp.exp(-rate * lax.broadcasted_iota(jnp.int32, (BLK, HEAD_DIM), 0).astype(F32))
    for b in range(blocks):
        rows = slice(b * BLK, (b + 1) * BLK)
        scores = dot(query_ref[rows, :], key_ref[rows, :], ((1,), (1,)))
        mixing = (scores * weight).astype(BF16)
        out_ref[rows, :] = dot(mixing, value_ref[rows, :], ((1,), (0,)))


def span_weight(rate, gap, span):
    wide = jnp.full((8, HEAD_DIM), jnp.maximum(gap, 0).astype(F32) * span, F32)
    return jnp.where(gap >= 0, jnp.exp(-rate * wide), 0.0)[:1, :]


def total_kernel(who, rate_ref, after_ref, *refs, group, heads, span):
    slots, out = refs[:group], refs[group]
    me = who[0]
    for h in range(heads):
        rate = rate_ref[me * heads + h]
        rows = slice(h * HEAD_DIM, (h + 1) * HEAD_DIM)
        total = None
        for e in range(group):
            part = span_weight(rate, group - 1 - (me ^ e), span) * slots[e][rows, :]
            total = part if total is None else total + part
        out[rows, :] = total


def carry_kernel(who, rate_ref, before_ref, *refs, group, heads, span):
    slots, outs = refs[:group], refs[group:]
    me = who[0]
    for h in range(heads):
        rate = rate_ref[me * heads + h]
        rows = slice(h * HEAD_DIM, (h + 1) * HEAD_DIM)
        parts = [slots[e][rows, :] for e in range(group)]
        before = before_ref[rows, :]
        for d in range(group):
            carry = span_weight(rate, me ^ d, span) * before
            for e in range(group):
                if e != d:
                    carry = carry + span_weight(rate, (me ^ d) - (me ^ e) - 1, span) * parts[e]
            outs[d][rows, :] = carry


def split_bf16(value):
    high = value.astype(BF16)
    rest = value - high.astype(F32)
    middle = rest.astype(BF16)
    return high, middle, (rest - middle.astype(F32)).astype(BF16)


def carried_kernel(who, rate_ref, query_ref, local_ref, terms_ref, inner_ref, *refs, group, blocks, heads):
    carries, att_ref, squares_ref, acc_ref = refs[:group], refs[group], refs[group + 1], refs[group + 2]
    for d in range(group):
        owner = who[0] ^ d
        part = heads * HEAD_DIM
        for h in range(heads):
            head = owner * heads + h
            rate = rate_ref[head]
            here = slice(h * HEAD_DIM, (h + 1) * HEAD_DIM)
            cols = pl.ds(pl.multiple_of(owner * part + h * HEAD_DIM, HEAD_DIM), HEAD_DIM)
            block_decay = jnp.exp(jnp.full((8, HEAD_DIM), -rate * BLK, F32))[:1, :]
            state = carries[d][here, :]
            for b in range(blocks):
                rows = slice(b * BLK, (b + 1) * BLK)
                carried = dot(query_ref[rows, cols], state.astype(BF16), ((1,), (0,)))
                att = local_ref[rows, cols] + carried * inner_ref[head]
                att_ref[rows, cols] = att
                if d == 0 and h == 0:
                    acc_ref[rows, :] = att * att
                else:
                    acc_ref[rows, :] += att * att
                if b < blocks - 1:
                    state = block_decay * state + terms_ref[b, d, here, :]
    ones = jnp.ones((8, HEAD_DIM), BF16)
    total = None
    for piece in split_bf16(acc_ref[...]):
        add = dot(ones, piece, ((1,), (1,)))
        total = add if total is None else total + add
    squares_ref[...] = total[:1, :]


def norm_kernel(*refs, features, count):
    squares, gain_ref, att_ref, out_ref, column_ref = refs[:count], *refs[count:]
    step = pl.program_id(0)

    @pl.when(step == 0)
    def _():
        total = squares[0][...]
        for other in squares[1:]:
            total = total + other[...]
        inverse = lax.rsqrt(total / features + 1e-06)
        row = lax.broadcasted_iota(jnp.int32, (16, inverse.shape[1]), 0)
        pieces = jnp.zeros(row.shape, F32)
        for i, piece in enumerate(split_bf16(inverse)):
            pieces = jnp.where(row == i, piece.astype(F32), pieces)
        column_ref[...] = dot(pieces.astype(BF16), jnp.ones((16, HEAD_DIM), BF16), ((0,), (0,)))

    height = out_ref.shape[0]
    rows = pl.ds(pl.multiple_of(step * height, height), height)
    column = column_ref[rows, :]
    for c in range(out_ref.shape[1] // HEAD_DIM):
        cols = slice(c * HEAD_DIM, (c + 1) * HEAD_DIM)
        out_ref[:, cols] = (att_ref[rows, cols] * column * gain_ref[:, cols]).astype(BF16)


def local(queries, key_vectors, value_vectors, decay_rate, norm_gain, *, zp, nc, ne, nt):
    rows, width = queries.shape
    heads_all = width // HEAD_DIM
    blocks = rows // BLK
    group = zp * ne
    heads = heads_all // group
    part = heads * HEAD_DIM
    z, x = lax.axis_index("ctx"), lax.axis_index("exp")
    who = jnp.reshape((z % zp) * ne + x, (1,)).astype(jnp.int32)
    smem = pl.BlockSpec(memory_space=pltpu.SMEM)
    vmem = pl.BlockSpec(memory_space=pltpu.VMEM)
    hbm = pl.BlockSpec(memory_space=pltpu.HBM)
    state_type = jax.ShapeDtypeStruct((part, HEAD_DIM), F32)
    order = list(range(1, group))

    *slots, terms = pl.pallas_call(
        functools.partial(spread_kernel, group=group, blocks=blocks, heads=heads, order=order + [0]),
        in_specs=[smem, hbm, hbm, hbm],
        out_specs=[vmem] * (group + 1),
        out_shape=[state_type] * group + [jax.ShapeDtypeStruct((max(blocks - 1, 1), group, part, HEAD_DIM), F32)],
        scratch_shapes=[
            pltpu.SMEM((heads_all,), F32),
            pltpu.VMEM((group, rows, part), BF16),
            pltpu.VMEM((group, rows, part), BF16),
            pltpu.SemaphoreType.DMA((2, group)),
            pltpu.SemaphoreType.DMA,
        ],
        compiler_params=params(),
        name="spread",
    )(who, *(pltpu.with_memory_space_constraint(a, pltpu.HBM) for a in (decay_rate, key_vectors, value_vectors)))

    def swap(value, d):
        pairs = []
        for zz in range(nc):
            for xx in range(ne):
                m = ((zz % zp) * ne + xx) ^ d
                pairs.append((zz * ne + xx, (zz // zp * zp + m // ne) * ne + m % ne))
        return lax.ppermute(value, ("ctx", "exp"), pairs)

    got = {d: swap(slots[d], d) for d in order}
    slots = [slots[0]] + [got[d] for d in range(1, group)]

    one_head = pl.BlockSpec((rows, HEAD_DIM), lambda h: (0, h))
    local_part, inner = pl.pallas_call(
        functools.partial(local_kernel, blocks=blocks),
        grid=(heads_all,),
        in_specs=[smem, one_head, one_head, one_head],
        out_specs=[one_head, pl.BlockSpec((1, BLK, HEAD_DIM), lambda h: (h, 0, 0))],
        out_shape=[jax.ShapeDtypeStruct((rows, width), F32), jax.ShapeDtypeStruct((heads_all, BLK, HEAD_DIM), F32)],
        compiler_params=params(),
        cost_estimate=pl.CostEstimate(flops=4 * rows * BLK * width, bytes_accessed=10 * rows * width, transcendentals=0),
        name="local_part",
    )(decay_rate, queries, key_vectors, value_vectors)

    span = float(rows)
    total = pl.pallas_call(
        functools.partial(total_kernel, group=group, heads=heads, span=span),
        in_specs=[smem, smem, pl.BlockSpec(memory_space=pl.ANY)] + [vmem] * group,
        out_specs=vmem,
        out_shape=state_type,
        compiler_params=params(),
        name="group_total",
    )(who, decay_rate, inner, *slots)
    groups = nc // zp
    before = lax.ppermute(total, "ctx", [(zz, zz + zp) for zz in range(nc - zp)])
    step = 1
    while step < groups - 1:
        rates = lax.dynamic_slice_in_dim(decay_rate, who[0] * heads, heads)
        scale = jnp.repeat(jnp.exp(-rates * (span * group * step)), HEAD_DIM)[:, None]
        moved = lax.ppermute(before, "ctx", [(zz, zz + zp * step) for zz in range(nc - zp * step)])
        before = before + scale * moved
        step *= 2

    carries = pl.pallas_call(
        functools.partial(carry_kernel, group=group, heads=heads, span=span),
        in_specs=[smem, smem] + [vmem] * (group + 1),
        out_specs=[vmem] * group,
        out_shape=[state_type] * group,
        compiler_params=params(),
        name="carry",
    )(who, decay_rate, before, *slots)
    got = {d: swap(carries[d], d) for d in order}
    carries = [carries[0]] + [got[d] for d in range(1, group)]

    attended, squares = pl.pallas_call(
        functools.partial(carried_kernel, group=group, blocks=blocks, heads=heads),
        in_specs=[smem, smem] + [vmem] * (4 + group),
        out_specs=[vmem, vmem],
        out_shape=[jax.ShapeDtypeStruct((rows, width), F32), jax.ShapeDtypeStruct((1, rows), F32)],
        scratch_shapes=[pltpu.VMEM((rows, HEAD_DIM), F32)],
        compiler_params=params(),
        name="carried",
    )(who, decay_rate, queries, local_part, terms, inner, *carries)

    if nt & (nt - 1) == 0:
        swaps = [[(i, i ^ d) for i in range(nt)] for d in range(1, nt)]
    else:
        swaps = [[(i, (i + d) % nt) for i in range(nt)] for d in range(1, nt)]
    sums = [squares] + [lax.ppermute(squares, "tp", pairs) for pairs in swaps[::-1]]

    height = rows // 4
    return pl.pallas_call(
        functools.partial(norm_kernel, features=float(width * nt), count=nt),
        grid=(rows // height,),
        in_specs=[vmem] * (nt + 2),
        out_specs=pl.BlockSpec((height, width), lambda i: (i, 0)),
        out_shape=jax.ShapeDtypeStruct((rows, width), BF16),
        scratch_shapes=[pltpu.VMEM((rows, HEAD_DIM), F32)],
        compiler_params=params(),
        name="norm",
    )(*sums, norm_gain[None, :], attended)


def solution(mesh):
    nc, ne, nt = mesh.shape["ctx"], mesh.shape["exp"], mesh.shape["tp"]

    def whole(queries, key_vectors, value_vectors, decay_rate, norm_gain):
        heads_local = decay_rate.shape[0] // nt
        zp = 2 if nc % 2 == 0 and heads_local % (2 * ne) == 0 else 1
        return jax.shard_map(
            functools.partial(local, zp=zp, nc=nc, ne=ne, nt=nt),
            mesh=mesh,
            in_specs=(P(("ctx", "exp"), "tp"),) * 3 + (P("tp"), P("tp")),
            out_specs=P(("ctx", "exp"), "tp"),
            check_vma=False,
        )(queries, key_vectors, value_vectors, decay_rate, norm_gain)

    return whole
```

```python
import functools
import jax
import jax.numpy as jnp
from jax import lax
from jax.experimental import pallas as pl
from jax.experimental.pallas import tpu as pltpu
from jax.sharding import PartitionSpec as P

HEAD_DIM = 128
BLK = 256
F32 = jnp.float32
BF16 = jnp.bfloat16


def dot(a, b, dims):
    return lax.dot_general(a, b, (dims, ((), ())), preferred_element_type=F32)


def params(mib=32):
    return pltpu.CompilerParams(vmem_limit_bytes=mib << 20)


def head_rows(h):
    return slice(h * HEAD_DIM, (h + 1) * HEAD_DIM)


def split_bf16(value):
    high = value.astype(BF16)
    rest = value - high.astype(F32)
    middle = rest.astype(BF16)
    return high, middle, (rest - middle.astype(F32)).astype(BF16)


def member(zp, ne):
    return (lax.axis_index("ctx") % zp) * ne + lax.axis_index("exp")


def load_kernel(rate_hbm, query_hbm, key_hbm, value_hbm, rates_ref, query_ref, key_ref, value_ref, rate_smem, sems, *, zp, ne, heads, order):
    me = member(zp, ne)
    part = heads * HEAD_DIM
    copies = []
    for n, (source, held) in enumerate(((key_hbm, key_ref), (value_hbm, value_ref), (query_hbm, query_ref))):
        for d in order:
            cols = pl.ds(pl.multiple_of((me ^ d) * part, part), part)
            copies.append(pltpu.make_async_copy(source.at[:, cols], held.at[d], sems.at[n, d]))
    rate_copy = pltpu.make_async_copy(rate_hbm, rate_smem, sems.at[3, 0])
    rate_copy.start()
    for copy in copies:
        copy.start()
    rate_copy.wait()
    for d in order:
        for h in range(heads):
            rates_ref[d, h] = jnp.full((8, HEAD_DIM), rate_smem[(me ^ d) * heads + h], F32)
    for copy in copies:
        copy.wait()


def spread_kernel(rates_ref, key_ref, value_ref, state_ref, terms_ref, *, d, blocks, heads):
    left = (BLK - lax.broadcasted_iota(jnp.int32, (BLK, HEAD_DIM), 0)).astype(F32)
    for h in range(heads):
        here = head_rows(h)
        rate = rates_ref[d, h][:1, :]
        tail = jnp.exp(-rate * left)
        block_decay = jnp.exp(-rate * BLK)
        own = None
        for b in range(blocks):
            rows = slice(b * BLK, (b + 1) * BLK)
            keys = (key_ref[d, rows, here].astype(F32) * tail).astype(BF16)
            term = dot(keys, value_ref[d, rows, here], ((0,), (0,)))
            if b < blocks - 1:
                terms_ref[b, here, :] = term
            own = term if own is None else block_decay * own + term
        state_ref[here, :] = own


def local_kernel(rates_ref, query_ref, key_ref, value_ref, out_ref, inner_ref, *, blocks, heads, group):
    sub = HEAD_DIM
    count = BLK // sub
    i = lax.broadcasted_iota(jnp.int32, (sub, sub), 0)
    j = lax.broadcasted_iota(jnp.int32, (sub, sub), 1)
    apart = (i - j).astype(F32)
    offset = lax.broadcasted_iota(jnp.int32, (BLK, HEAD_DIM), 0).astype(F32)
    for d in range(group):
        for h in range(heads):
            rate = rates_ref[d, h][:1, :]
            weights = [jnp.where(apart >= 0, jnp.exp(-rate * jnp.maximum(apart, 0.0)), 0.0)]
            weights += [jnp.exp(-rate * (apart + float(sub * n))) for n in range(1, count)]
            inner_ref[d, h] = jnp.exp(-rate * offset)
            cols = head_rows(h)
            for b in range(blocks):
                for n in range(count):
                    rows = slice(b * BLK + n * sub, b * BLK + (n + 1) * sub)
                    seen = slice(b * BLK, b * BLK + (n + 1) * sub)
                    scores = dot(query_ref[d, rows, cols], key_ref[d, seen, cols], ((1,), (1,)))
                    weight = weights[0] if n == 0 else jnp.concatenate(weights[n::-1], axis=1)
                    mixing = (scores * weight).astype(BF16)
                    out_ref[d, rows, cols] = dot(mixing, value_ref[d, seen, cols], ((1,), (0,)))


def span_weight(rate, gap, span):
    return jnp.where(gap >= 0, jnp.exp(-rate * (jnp.maximum(gap, 0).astype(F32) * span)), 0.0)


def total_kernel(rates_ref, after_ref, *refs, ring, heads, span, zp, ne):
    group = len(ring)
    slots, out = refs[:group], refs[group]
    me = member(zp, ne)
    for h in range(heads):
        rate = rates_ref[0, h][:1, :]
        total = None
        for e, slot in zip(ring, slots):
            part = span_weight(rate, group - 1 - (me ^ e), span) * slot[head_rows(h), :]
            total = part if total is None else total + part
        out[head_rows(h), :] = total


def carry_kernel(rates_ref, before_ref, *refs, ring, heads, span, zp, ne):
    group = len(ring)
    slots, outs = refs[:group], refs[group:]
    me = member(zp, ne)
    has_before = lax.axis_index("ctx") >= zp
    for h in range(heads):
        rate = rates_ref[0, h][:1, :]
        parts = [slot[head_rows(h), :] for slot in slots]
        before = jnp.where(has_before, before_ref[head_rows(h), :], 0.0)
        for d, out in zip(ring, outs):
            carry = span_weight(rate, me ^ d, span) * before
            for e, part in zip(ring, parts):
                if e != d:
                    carry = carry + span_weight(rate, (me ^ d) - (me ^ e) - 1, span) * part
            out[head_rows(h), :] = carry


def carried_kernel(rates_ref, query_ref, local_ref, inner_ref, *refs, ds, blocks, heads):
    count = len(ds)
    terms, carries, (att_ref, acc_ref) = refs[:count], refs[count : 2 * count], refs[2 * count :]
    for i, d in enumerate(ds):
        for h in range(heads):
            here = head_rows(h)
            block_decay = jnp.exp(-rates_ref[d, h][:1, :] * BLK)
            state = carries[i][here, :]
            for b in range(blocks):
                rows = slice(b * BLK, (b + 1) * BLK)
                carried = dot(query_ref[d, rows, here], state.astype(BF16), ((1,), (0,)))
                att = local_ref[d, rows, here] + carried * inner_ref[d, h]
                att_ref[i, rows, here] = att
                if i == 0 and h == 0:
                    acc_ref[rows, :] = att * att
                else:
                    acc_ref[rows, :] += att * att
                if b < blocks - 1:
                    state = block_decay * state + terms[i][b, here, :]


def squares_kernel(*refs):
    parts, out_ref = refs[:-1], refs[-1]
    squares = parts[0][...]
    for other in parts[1:]:
        squares = squares + other[...]
    ones = jnp.ones((8, HEAD_DIM), BF16)
    total = None
    for piece in split_bf16(squares):
        add = dot(ones, piece, ((1,), (1,)))
        total = add if total is None else total + add
    out_ref[...] = total[:1, :]


def norm_kernel(*refs, features, count, steps, parts, zp, ne, heads):
    squares, gain_ref, refs = refs[:count], refs[count], refs[count + 1 :]
    atts, (out_hbm, out_ref, column_ref, sems) = refs[: len(parts)], refs[len(parts) :]
    me = member(zp, ne)
    total = squares[0][...]
    for other in squares[1:]:
        total = total + other[...]
    inverse = lax.rsqrt(total / features + 1e-06)
    row = lax.broadcasted_iota(jnp.int32, (16, inverse.shape[1]), 0)
    pieces = jnp.zeros(row.shape, F32)
    for i, piece in enumerate(split_bf16(inverse)):
        pieces = jnp.where(row == i, piece.astype(F32), pieces)
    column_ref[...] = dot(pieces.astype(BF16), jnp.ones((16, HEAD_DIM), BF16), ((0,), (0,)))
    height = out_ref.shape[0] // steps
    copies = []
    for step in range(steps):
        rows = slice(step * height, (step + 1) * height)
        column = column_ref[rows, :]
        for att, ds in zip(atts, parts):
            for i, d in enumerate(ds):
                for h in range(heads):
                    cols = pl.ds(pl.multiple_of(((me ^ d) * heads + h) * HEAD_DIM, HEAD_DIM), HEAD_DIM)
                    out_ref[rows, cols] = (att[i, rows, head_rows(h)] * column * gain_ref[:, cols]).astype(BF16)
        copies.append(pltpu.make_async_copy(out_ref.at[rows, :], out_hbm.at[rows, :], sems.at[step]))
        copies[-1].start()
    for copy in copies:
        copy.wait()


def local(queries, key_vectors, value_vectors, decay_rate, norm_gain, *, zp, nc, ne, nt):
    rows, width = queries.shape
    heads_all = width // HEAD_DIM
    blocks = rows // BLK
    group = zp * ne
    groups = nc // zp
    heads = heads_all // group
    part = heads * HEAD_DIM
    span = float(rows)
    vmem = pl.BlockSpec(memory_space=pltpu.VMEM)
    hbm = pl.BlockSpec(memory_space=pltpu.HBM)
    anywhere = pl.BlockSpec(memory_space=pl.ANY)
    ring = (0, 3, 2, 1) if group == 4 else tuple(range(group))
    state_type = jax.ShapeDtypeStruct((part, HEAD_DIM), F32)
    term_type = jax.ShapeDtypeStruct((max(blocks - 1, 1), part, HEAD_DIM), F32)
    held_type = jax.ShapeDtypeStruct((group, rows, part), BF16)
    where = dict(zp=zp, ne=ne)

    def call(kernel, count, outs, name, **more):
        more = {"in_specs": [vmem] * count, "out_specs": [vmem] * len(outs), "out_shape": outs, "name": name, **more}
        return pl.pallas_call(kernel, compiler_params=params(), **more)

    pinned = [pltpu.with_memory_space_constraint(a, pltpu.HBM) for a in (decay_rate, queries, key_vectors, value_vectors)]
    order = ring[1:] + ring[:1]
    rates, query, key, value = call(
        functools.partial(load_kernel, heads=heads, order=order, **where),
        4,
        [jax.ShapeDtypeStruct((group, heads, 8, HEAD_DIM), F32), held_type, held_type, held_type],
        "load",
        in_specs=[hbm] * 4,
        scratch_shapes=[pltpu.SMEM((heads_all,), F32), pltpu.SemaphoreType.DMA((4, group))],
    )(*pinned)

    slots, terms = {}, {}
    for d in order:
        spread = functools.partial(spread_kernel, d=d, blocks=blocks, heads=heads)
        slots[d], terms[d] = call(spread, 3, [state_type, term_type], "spread")(rates, key, value)

    def swap(value, d):
        pairs = []
        for zz in range(nc):
            for xx in range(ne):
                m = ((zz % zp) * ne + xx) ^ d
                pairs.append((zz * ne + xx, (zz // zp * zp + m // ne) * ne + m % ne))
        return lax.ppermute(value, ("ctx", "exp"), pairs)

    slots = [slots[0]] + [swap(slots[d], d) for d in ring[1:]]

    local_part, inner = call(
        functools.partial(local_kernel, blocks=blocks, heads=heads, group=group),
        4,
        [jax.ShapeDtypeStruct((group, rows, part), F32), jax.ShapeDtypeStruct((group, heads, BLK, HEAD_DIM), F32)],
        "local_part",
        cost_estimate=pl.CostEstimate(flops=4 * rows * BLK * width, bytes_accessed=10 * rows * width, transcendentals=0),
    )(rates, query, key, value)

    (total,) = call(
        functools.partial(total_kernel, ring=ring, heads=heads, span=span, **where),
        group + 2,
        [state_type],
        "group_total",
        in_specs=[vmem, anywhere] + [vmem] * group,
    )(rates, inner, *slots)

    if groups == 2:
        before = lax.ppermute(total, "ctx", [(zz, (zz + zp) % nc) for zz in range(nc)])
    else:
        before = lax.ppermute(total, "ctx", [(zz, zz + zp) for zz in range(nc - zp)])
    step = 1
    while step < groups - 1:
        scale = jnp.exp(-rates[0, :, :1, :] * (span * group * step))
        moved = lax.ppermute(before, "ctx", [(zz, zz + zp * step) for zz in range(nc - zp * step)])
        before = before + (scale * moved.reshape(heads, HEAD_DIM, HEAD_DIM)).reshape(part, HEAD_DIM)
        step *= 2

    carries = call(
        functools.partial(carry_kernel, ring=ring, heads=heads, span=span, **where), group + 2, [state_type] * group, "carry"
    )(rates, before, *slots)
    carries = [carries[0]] + [swap(carry, d) for carry, d in zip(carries[1:], ring[1:])]

    parts = [(d,) for d in ring]
    attended, squares, at = [], [], 0
    for ds in parts:
        att, acc = call(
            functools.partial(carried_kernel, ds=ds, blocks=blocks, heads=heads),
            4 + 2 * len(ds),
            [jax.ShapeDtypeStruct((len(ds), rows, part), F32), jax.ShapeDtypeStruct((rows, HEAD_DIM), F32)],
            "carried",
        )(rates, query, local_part, inner, *(terms[d] for d in ds), *carries[at : at + len(ds)])
        attended.append(att)
        squares.append(acc)
        at += len(ds)
    (row_sum,) = call(squares_kernel, len(parts), [jax.ShapeDtypeStruct((1, rows), F32)], "row_squares")(*squares)

    if nt & (nt - 1) == 0:
        swaps = [[(i, i ^ d) for i in range(nt)] for d in range(1, nt)]
    else:
        swaps = [[(i, (i + d) % nt) for i in range(nt)] for d in range(1, nt)]
    row_sums = [row_sum] + [lax.ppermute(row_sum, "tp", pairs) for pairs in swaps[::-1]]

    steps = 4
    norm = functools.partial(norm_kernel, features=float(width * nt), count=nt, steps=steps, parts=parts, heads=heads, **where)
    (out,) = call(
        norm,
        nt + 1 + len(parts),
        [jax.ShapeDtypeStruct((rows, width), BF16)],
        "norm",
        out_specs=[hbm],
        scratch_shapes=[
            pltpu.VMEM((rows, width), BF16),
            pltpu.VMEM((rows, HEAD_DIM), F32),
            pltpu.SemaphoreType.DMA((steps,)),
        ],
    )(*row_sums, norm_gain[None, :], *attended)
    return out


def solution(mesh):
    nc, ne, nt = mesh.shape["ctx"], mesh.shape["exp"], mesh.shape["tp"]

    def whole(queries, key_vectors, value_vectors, decay_rate, norm_gain):
        heads_local = decay_rate.shape[0] // nt
        zp = 2 if nc % 2 == 0 and heads_local % (2 * ne) == 0 else 1
        return jax.shard_map(
            functools.partial(local, zp=zp, nc=nc, ne=ne, nt=nt),
            mesh=mesh,
            in_specs=(P(("ctx", "exp"), "tp"),) * 3 + (P("tp"), P("tp")),
            out_specs=P(("ctx", "exp"), "tp"),
            check_vma=False,
        )(queries, key_vectors, value_vectors, decay_rate, norm_gain)

    return whole
```

```python
import functools
import jax
import jax.numpy as jnp
from jax import lax
from jax.experimental import pallas as pl
from jax.experimental.pallas import tpu as pltpu
from jax.sharding import PartitionSpec as P

HEAD_DIM = 128
BLK = 256
F32 = jnp.float32
BF16 = jnp.bfloat16


def dot(a, b, dims):
    return lax.dot_general(a, b, (dims, ((), ())), preferred_element_type=F32)


def params(mib=32):
    return pltpu.CompilerParams(vmem_limit_bytes=mib << 20)


def head_rows(h):
    return slice(h * HEAD_DIM, (h + 1) * HEAD_DIM)


def split_bf16(value):
    high = value.astype(BF16)
    rest = value - high.astype(F32)
    middle = rest.astype(BF16)
    return high, middle, (rest - middle.astype(F32)).astype(BF16)


def member(zp, ne):
    return (lax.axis_index("ctx") % zp) * ne + lax.axis_index("exp")


def owned(zp, ne, mirror):
    me = member(zp, ne)
    return me ^ (lax.axis_index("ctx") // zp % 2 * ne) if mirror else me


def load_kernel(rate_hbm, query_hbm, key_hbm, value_hbm, rates_ref, query_ref, key_ref, value_ref, rate_smem, sems, *, zp, ne, mirror, heads, order):
    me = owned(zp, ne, mirror)
    part = heads * HEAD_DIM
    copies = []
    for n, (source, held) in enumerate(((key_hbm, key_ref), (value_hbm, value_ref), (query_hbm, query_ref))):
        for d in order:
            cols = pl.ds(pl.multiple_of((me ^ d) * part, part), part)
            copies.append(pltpu.make_async_copy(source.at[:, cols], held.at[d], sems.at[n, d]))
    rate_copy = pltpu.make_async_copy(rate_hbm, rate_smem, sems.at[3, 0])
    rate_copy.start()
    for copy in copies:
        copy.start()
    rate_copy.wait()
    for d in order:
        for h in range(heads):
            rates_ref[d, h] = jnp.full((8, HEAD_DIM), rate_smem[(me ^ d) * heads + h], F32)
    for copy in copies:
        copy.wait()


def spread_kernel(rates_ref, key_ref, value_ref, state_ref, terms_ref, *, d, blocks, heads):
    left = (BLK - lax.broadcasted_iota(jnp.int32, (BLK, HEAD_DIM), 0)).astype(F32)
    for h in range(heads):
        here = head_rows(h)
        rate = rates_ref[d, h][:1, :]
        tail = jnp.exp(-rate * left)
        block_decay = jnp.exp(-rate * BLK)
        own = None
        for b in range(blocks):
            rows = slice(b * BLK, (b + 1) * BLK)
            keys = (key_ref[d, rows, here].astype(F32) * tail).astype(BF16)
            term = dot(keys, value_ref[d, rows, here], ((0,), (0,)))
            if b < blocks - 1:
                terms_ref[b, here, :] = term
            own = term if own is None else block_decay * own + term
        state_ref[here, :] = own


def local_kernel(rates_ref, query_ref, key_ref, value_ref, out_ref, inner_ref, *, blocks, heads, group):
    sub = HEAD_DIM
    count = BLK // sub
    i = lax.broadcasted_iota(jnp.int32, (sub, sub), 0)
    j = lax.broadcasted_iota(jnp.int32, (sub, sub), 1)
    apart = (i - j).astype(F32)
    offset = lax.broadcasted_iota(jnp.int32, (BLK, HEAD_DIM), 0).astype(F32)
    for d in range(group):
        for h in range(heads):
            rate = rates_ref[d, h][:1, :]
            weights = [jnp.where(apart >= 0, jnp.exp(-rate * jnp.maximum(apart, 0.0)), 0.0)]
            weights += [jnp.exp(-rate * (apart + float(sub * n))) for n in range(1, count)]
            inner_ref[d, h] = jnp.exp(-rate * offset)
            cols = head_rows(h)
            for b in range(blocks):
                for n in range(count):
                    rows = slice(b * BLK + n * sub, b * BLK + (n + 1) * sub)
                    seen = slice(b * BLK, b * BLK + (n + 1) * sub)
                    scores = dot(query_ref[d, rows, cols], key_ref[d, seen, cols], ((1,), (1,)))
                    weight = weights[0] if n == 0 else jnp.concatenate(weights[n::-1], axis=1)
                    mixing = (scores * weight).astype(BF16)
                    out_ref[d, rows, cols] = dot(mixing, value_ref[d, seen, cols], ((1,), (0,)))


def span_weight(rate, gap, span):
    return jnp.where(gap >= 0, jnp.exp(-rate * (jnp.maximum(gap, 0).astype(F32) * span)), 0.0)


def total_kernel(rates_ref, after_ref, *refs, ring, heads, span, zp, ne):
    group = len(ring)
    slots, out = refs[:group], refs[group]
    me = member(zp, ne)
    for h in range(heads):
        rate = rates_ref[0, h][:1, :]
        total = None
        for e, slot in zip(ring, slots):
            part = span_weight(rate, group - 1 - (me ^ e), span) * slot[head_rows(h), :]
            total = part if total is None else total + part
        out[head_rows(h), :] = total


def carry_kernel(rates_ref, before_ref, *refs, ring, ring_out, heads, span, zp, ne):
    group = len(ring)
    slots, outs = refs[:group], refs[group:]
    me = member(zp, ne)
    has_before = lax.axis_index("ctx") >= zp
    for h in range(heads):
        rate = rates_ref[0, h][:1, :]
        parts = [slot[head_rows(h), :] for slot in slots]
        before = jnp.where(has_before, before_ref[head_rows(h), :], 0.0)
        for d, out in zip(ring_out, outs):
            carry = span_weight(rate, me ^ d, span) * before
            for e, part in zip(ring, parts):
                if e != d:
                    carry = carry + span_weight(rate, (me ^ d) - (me ^ e) - 1, span) * part
            out[head_rows(h), :] = carry


def carried_kernel(rates_ref, query_ref, local_ref, inner_ref, terms_ref, carry_ref, *refs, d, blocks, heads, first, last):
    earlier_ref = None if first else refs[0]
    att_ref, acc_ref = refs[0 if first else 1 :][:2]
    sums = []
    for h in range(heads):
        here = head_rows(h)
        block_decay = jnp.exp(-rates_ref[d, h][:1, :] * BLK)
        state = carry_ref[here, :]
        for b in range(blocks):
            rows = slice(b * BLK, (b + 1) * BLK)
            carried = dot(query_ref[d, rows, here], state.astype(BF16), ((1,), (0,)))
            att = local_ref[d, rows, here] + carried * inner_ref[d, h]
            att_ref[rows, here] = att
            square = att * att
            if h > 0:
                square = square + sums[b]
                sums[b] = square
            else:
                sums.append(square)
            if b < blocks - 1:
                state = block_decay * state + terms_ref[b, here, :]
    for b in range(blocks):
        rows = slice(b * BLK, (b + 1) * BLK)
        square = sums[b] if first else sums[b] + earlier_ref[rows, :]
        if last:
            ones = jnp.ones((8, HEAD_DIM), BF16)
            total = None
            for piece in split_bf16(square)[:2]:
                add = dot(ones, piece, ((1,), (1,)))
                total = add if total is None else total + add
            acc_ref[:, rows] = total[:1, :]
        else:
            acc_ref[rows, :] = square


def norm_kernel(*refs, features, count, steps, ring, zp, ne, mirror, heads):
    squares, gain_ref, refs = refs[:count], refs[count], refs[count + 1 :]
    atts, (out_hbm, out_ref, column_ref, sems) = refs[: len(ring)], refs[len(ring) :]
    me = owned(zp, ne, mirror)
    total = squares[0][...]
    for other in squares[1:]:
        total = total + other[...]
    inverse = lax.rsqrt(total / features + 1e-06)
    row = lax.broadcasted_iota(jnp.int32, (16, inverse.shape[1]), 0)
    pieces = jnp.zeros(row.shape, F32)
    for i, piece in enumerate(split_bf16(inverse)):
        pieces = jnp.where(row == i, piece.astype(F32), pieces)
    column_ref[...] = dot(pieces.astype(BF16), jnp.ones((16, HEAD_DIM), BF16), ((0,), (0,)))
    height = out_ref.shape[0] // steps
    copies = []
    for step in range(steps):
        rows = slice(step * height, (step + 1) * height)
        column = column_ref[rows, :]
        for att, d in zip(atts, ring):
            for h in range(heads):
                cols = pl.ds(pl.multiple_of(((me ^ d) * heads + h) * HEAD_DIM, HEAD_DIM), HEAD_DIM)
                out_ref[rows, cols] = (att[rows, head_rows(h)] * column * gain_ref[:, cols]).astype(BF16)
        copies.append(pltpu.make_async_copy(out_ref.at[rows, :], out_hbm.at[rows, :], sems.at[step]))
        copies[-1].start()
    for copy in copies:
        copy.wait()


def local(queries, key_vectors, value_vectors, decay_rate, norm_gain, *, zp, nc, ne, nt):
    rows, width = queries.shape
    heads_all = width // HEAD_DIM
    blocks = rows // BLK
    group = zp * ne
    groups = nc // zp
    heads = heads_all // group
    part = heads * HEAD_DIM
    span = float(rows)
    vmem = pl.BlockSpec(memory_space=pltpu.VMEM)
    hbm = pl.BlockSpec(memory_space=pltpu.HBM)
    anywhere = pl.BlockSpec(memory_space=pl.ANY)
    ring = (0, 1, 2, 3) if group == 4 else tuple(range(group))
    ring3 = (0, 2, 1, 3) if group == 4 else tuple(range(group))
    state_type = jax.ShapeDtypeStruct((part, HEAD_DIM), F32)
    term_type = jax.ShapeDtypeStruct((max(blocks - 1, 1), part, HEAD_DIM), F32)
    held_type = jax.ShapeDtypeStruct((group, rows, part), BF16)
    where = dict(zp=zp, ne=ne)
    mirror = groups == 2 and zp == 2

    def call(kernel, count, outs, name, **more):
        more = {"in_specs": [vmem] * count, "out_specs": [vmem] * len(outs), "out_shape": outs, "name": name, **more}
        return pl.pallas_call(kernel, compiler_params=params(), **more)

    pinned = [pltpu.with_memory_space_constraint(a, pltpu.HBM) for a in (decay_rate, queries, key_vectors, value_vectors)]
    order = ring[1:] + ring[:1]
    rates, query, key, value = call(
        functools.partial(load_kernel, heads=heads, order=order, mirror=mirror, **where),
        4,
        [jax.ShapeDtypeStruct((group, heads, 8, HEAD_DIM), F32), held_type, held_type, held_type],
        "load",
        in_specs=[hbm] * 4,
        scratch_shapes=[pltpu.SMEM((heads_all,), F32), pltpu.SemaphoreType.DMA((4, group))],
    )(*pinned)

    slots, terms = {}, {}
    for d in order:
        spread = functools.partial(spread_kernel, d=d, blocks=blocks, heads=heads)
        slots[d], terms[d] = call(spread, 3, [state_type, term_type], "spread")(rates, key, value)

    def swap(value, d):
        pairs = []
        for zz in range(nc):
            for xx in range(ne):
                m = ((zz % zp) * ne + xx) ^ d
                pairs.append((zz * ne + xx, (zz // zp * zp + m // ne) * ne + m % ne))
        return lax.ppermute(value, ("ctx", "exp"), pairs)

    slots = [slots[0]] + [swap(slots[d], d) for d in ring[1:]]

    local_part, inner = call(
        functools.partial(local_kernel, blocks=blocks, heads=heads, group=group),
        4,
        [jax.ShapeDtypeStruct((group, rows, part), F32), jax.ShapeDtypeStruct((group, heads, BLK, HEAD_DIM), F32)],
        "local_part",
        cost_estimate=pl.CostEstimate(flops=4 * rows * BLK * width, bytes_accessed=10 * rows * width, transcendentals=0),
    )(rates, query, key, value)

    (total,) = call(
        functools.partial(total_kernel, ring=ring, heads=heads, span=span, **where),
        group + 2,
        [state_type],
        "group_total",
        in_specs=[vmem, anywhere] + [vmem] * group,
    )(rates, inner, *slots)

    if groups == 2:
        before = lax.ppermute(total, "ctx", [(zz, nc - 1 - zz if mirror else (zz + zp) % nc) for zz in range(nc)])
    else:
        before = lax.ppermute(total, "ctx", [(zz, zz + zp) for zz in range(nc - zp)])
    step = 1
    while step < groups - 1:
        scale = jnp.exp(-rates[0, :, :1, :] * (span * group * step))
        moved = lax.ppermute(before, "ctx", [(zz, zz + zp * step) for zz in range(nc - zp * step)])
        before = before + (scale * moved.reshape(heads, HEAD_DIM, HEAD_DIM)).reshape(part, HEAD_DIM)
        step *= 2

    carries = call(
        functools.partial(carry_kernel, ring=ring, ring_out=ring3, heads=heads, span=span, **where), group + 2, [state_type] * group, "carry"
    )(rates, before, *slots)
    carries = [carries[0]] + [swap(carry, d) for carry, d in zip(carries[1:], ring3[1:])]

    attended, row_sum = [], None
    for i, d in enumerate(ring3):
        first, last = i == 0, i == group - 1
        att, row_sum = call(
            functools.partial(carried_kernel, d=d, blocks=blocks, heads=heads, first=first, last=last),
            6 if first else 7,
            [jax.ShapeDtypeStruct((rows, part), F32), jax.ShapeDtypeStruct((1, rows) if last else (rows, HEAD_DIM), F32)],
            "carried",
        )(rates, query, local_part, inner, terms[d], carries[i], *([] if first else [row_sum]))
        attended.append(att)

    if nt & (nt - 1) == 0:
        swaps = [[(i, i ^ d) for i in range(nt)] for d in range(1, nt)]
    else:
        swaps = [[(i, (i + d) % nt) for i in range(nt)] for d in range(1, nt)]
    row_sums = [row_sum] + [lax.ppermute(row_sum, "tp", pairs) for pairs in swaps]

    steps = 4
    norm = functools.partial(norm_kernel, features=float(width * nt), count=nt, steps=steps, ring=ring3, heads=heads, mirror=mirror, **where)
    (out,) = call(
        norm,
        nt + 1 + group,
        [jax.ShapeDtypeStruct((rows, width), BF16)],
        "norm",
        out_specs=[hbm],
        scratch_shapes=[
            pltpu.VMEM((rows, width), BF16),
            pltpu.VMEM((rows, HEAD_DIM), F32),
            pltpu.SemaphoreType.DMA((steps,)),
        ],
    )(*row_sums, norm_gain[None, :], *attended)
    return out


def solution(mesh):
    nc, ne, nt = mesh.shape["ctx"], mesh.shape["exp"], mesh.shape["tp"]

    def whole(queries, key_vectors, value_vectors, decay_rate, norm_gain):
        heads_local = decay_rate.shape[0] // nt
        zp = 2 if nc % 2 == 0 and heads_local % (2 * ne) == 0 else 1
        return jax.shard_map(
            functools.partial(local, zp=zp, nc=nc, ne=ne, nt=nt),
            mesh=mesh,
            in_specs=(P(("ctx", "exp"), "tp"),) * 3 + (P("tp"), P("tp")),
            out_specs=P(("ctx", "exp"), "tp"),
            check_vma=False,
        )(queries, key_vectors, value_vectors, decay_rate, norm_gain)

    return whole
```

```python
import functools
import jax
import jax.numpy as jnp
from jax import lax
from jax.experimental import pallas as pl
from jax.experimental.pallas import tpu as pltpu
from jax.sharding import PartitionSpec as P

HEAD_DIM = 128
BLK = 256
F32 = jnp.float32
BF16 = jnp.bfloat16


def dot(a, b, dims):
    return lax.dot_general(a, b, (dims, ((), ())), preferred_element_type=F32)


def params(mib=32):
    return pltpu.CompilerParams(vmem_limit_bytes=mib << 20)


def head_rows(h):
    return slice(h * HEAD_DIM, (h + 1) * HEAD_DIM)


def member(zp, ne):
    return (lax.axis_index("ctx") % zp) * ne + lax.axis_index("exp")


def owned(zp, ne, mirror):
    me = member(zp, ne)
    return me ^ (lax.axis_index("ctx") // zp % 2 * ne) if mirror else me


def spread(d, rate_of, key_ref, value_ref, state_ref, terms_ref, blocks, heads):
    left = (BLK - lax.broadcasted_iota(jnp.int32, (BLK, HEAD_DIM), 0)).astype(F32)
    for h in range(heads):
        here = head_rows(h)
        rate = rate_of(h)
        tail = jnp.exp(-rate * left)
        block_decay = jnp.exp(-rate * BLK)
        own = None
        for b in range(blocks):
            rows = slice(b * BLK, (b + 1) * BLK)
            keys = (key_ref[d, rows, here].astype(F32) * tail).astype(BF16)
            term = dot(keys, value_ref[d, rows, here], ((0,), (0,)))
            if b < blocks - 1:
                terms_ref[b, here, :] = term
            own = term if own is None else block_decay * own + term
        state_ref[here, :] = own


def load_kernel(rate_hbm, query_hbm, key_hbm, value_hbm, *refs, zp, ne, mirror, heads, blocks, order, early):
    rates_ref, query_ref, key_ref, value_ref = refs[:4]
    states, terms, (rate_smem, sems) = refs[4 : 4 + early], refs[4 + early : 4 + 2 * early], refs[4 + 2 * early :]
    me = owned(zp, ne, mirror)
    part = heads * HEAD_DIM

    def copy_of(n, d):
        source, held = ((key_hbm, key_ref), (value_hbm, value_ref), (query_hbm, query_ref))[n]
        cols = pl.ds(pl.multiple_of((me ^ d) * part, part), part)
        return pltpu.make_async_copy(source.at[:, cols], held.at[d], sems.at[n, d])

    rate_copy = pltpu.make_async_copy(rate_hbm, rate_smem, sems.at[3, 0])
    rate_copy.start()
    for d in order:
        copy_of(0, d).start()
        copy_of(1, d).start()
    for d in order:
        copy_of(2, d).start()
    rate_copy.wait()
    for d in order:
        for h in range(heads):
            rates_ref[d, h] = jnp.full((8, HEAD_DIM), rate_smem[(me ^ d) * heads + h], F32)
    for i, d in enumerate(order):
        copy_of(0, d).wait()
        copy_of(1, d).wait()
        if i < early:
            spread(d, lambda h: rates_ref[d, h][:1, :], key_ref, value_ref, states[i], terms[i], blocks, heads)
    for d in order:
        copy_of(2, d).wait()


def spread_kernel(rates_ref, key_ref, value_ref, state_ref, terms_ref, *, d, blocks, heads):
    spread(d, lambda h: rates_ref[d, h][:1, :], key_ref, value_ref, state_ref, terms_ref, blocks, heads)


def local_kernel(rates_ref, query_ref, key_ref, value_ref, out_ref, inner_ref, *, blocks, heads, group):
    sub = HEAD_DIM
    count = BLK // sub
    i = lax.broadcasted_iota(jnp.int32, (sub, sub), 0)
    j = lax.broadcasted_iota(jnp.int32, (sub, sub), 1)
    apart = (i - j).astype(F32)
    offset = lax.broadcasted_iota(jnp.int32, (BLK, HEAD_DIM), 0).astype(F32)
    for d in range(group):
        for h in range(heads):
            rate = rates_ref[d, h][:1, :]
            weights = [jnp.where(apart >= 0, jnp.exp(-rate * jnp.maximum(apart, 0.0)), 0.0)]
            weights += [jnp.exp(-rate * (apart + float(sub * n))) for n in range(1, count)]
            inner_ref[d, h] = jnp.exp(-rate * offset)
            cols = head_rows(h)
            for b in range(blocks):
                for n in range(count):
                    rows = slice(b * BLK + n * sub, b * BLK + (n + 1) * sub)
                    seen = slice(b * BLK, b * BLK + (n + 1) * sub)
                    scores = dot(query_ref[d, rows, cols], key_ref[d, seen, cols], ((1,), (1,)))
                    weight = weights[0] if n == 0 else jnp.concatenate(weights[n::-1], axis=1)
                    mixing = (scores * weight).astype(BF16)
                    out_ref[d, rows, cols] = dot(mixing, value_ref[d, seen, cols], ((1,), (0,)))


def span_weight(rate, gap, span):
    return jnp.where(gap >= 0, jnp.exp(-rate * (jnp.maximum(gap, 0).astype(F32) * span)), 0.0)


def total_kernel(rates_ref, after_ref, *refs, ring, heads, span, zp, ne):
    group = len(ring)
    slots, out = refs[:group], refs[group]
    me = member(zp, ne)
    for h in range(heads):
        rate = rates_ref[0, h][:1, :]
        total = None
        for e, slot in zip(ring, slots):
            part = span_weight(rate, group - 1 - (me ^ e), span) * slot[head_rows(h), :]
            total = part if total is None else total + part
        out[head_rows(h), :] = total


def carry_kernel(rates_ref, before_ref, *refs, ring, ring_out, heads, span, zp, ne):
    group = len(ring)
    slots, outs = refs[:group], refs[group:]
    me = member(zp, ne)
    has_before = lax.axis_index("ctx") >= zp
    for h in range(heads):
        rate = rates_ref[0, h][:1, :]
        parts = [slot[head_rows(h), :] for slot in slots]
        before = jnp.where(has_before, before_ref[head_rows(h), :], 0.0)
        for d, out in zip(ring_out, outs):
            carry = span_weight(rate, me ^ d, span) * before
            for e, part in zip(ring, parts):
                if e != d:
                    carry = carry + span_weight(rate, (me ^ d) - (me ^ e) - 1, span) * part
            out[head_rows(h), :] = carry


def carried_kernel(rates_ref, query_ref, local_ref, inner_ref, terms_ref, carry_ref, *refs, d, blocks, heads, first, last):
    earlier_ref = None if first else refs[0]
    att_ref, acc_ref = refs[0 if first else 1 :][:2]
    sums = []
    for h in range(heads):
        here = head_rows(h)
        block_decay = jnp.exp(-rates_ref[d, h][:1, :] * BLK)
        state = carry_ref[here, :]
        for b in range(blocks):
            rows = slice(b * BLK, (b + 1) * BLK)
            carried = dot(query_ref[d, rows, here], state.astype(BF16), ((1,), (0,)))
            att = local_ref[d, rows, here] + carried * inner_ref[d, h]
            att_ref[rows, here] = att
            square = att * att
            if h > 0:
                square = square + sums[b]
                sums[b] = square
            else:
                sums.append(square)
            if b < blocks - 1:
                state = block_decay * state + terms_ref[b, here, :]
    for b in range(blocks):
        rows = slice(b * BLK, (b + 1) * BLK)
        square = sums[b] if first else sums[b] + earlier_ref[rows, :]
        if last:
            for at in range(0, BLK, HEAD_DIM):
                turned = jnp.transpose(square[at : at + HEAD_DIM, :])
                acc_ref[:, b * BLK + at : b * BLK + at + HEAD_DIM] = jnp.sum(turned, axis=0, keepdims=True)
        else:
            acc_ref[rows, :] = square


def norm_kernel(*refs, features, count, steps, ring, zp, ne, mirror, heads):
    squares, gain_ref, refs = refs[:count], refs[count], refs[count + 1 :]
    atts, (out_hbm, out_ref, sems) = refs[: len(ring)], refs[len(ring) :]
    me = owned(zp, ne, mirror)
    total = squares[0][...]
    for other in squares[1:]:
        total = total + other[...]
    inverse = lax.rsqrt(total / features + 1e-06)
    height = out_ref.shape[0] // steps
    copies = []
    for step in range(steps):
        rows = slice(step * height, (step + 1) * height)
        tiles = [inverse[:, at : at + HEAD_DIM] for at in range(step * height, (step + 1) * height, HEAD_DIM)]
        column = jnp.concatenate([jnp.transpose(jnp.broadcast_to(tile, (HEAD_DIM, HEAD_DIM))) for tile in tiles], axis=0)
        for att, d in zip(atts, ring):
            for h in range(heads):
                cols = pl.ds(pl.multiple_of(((me ^ d) * heads + h) * HEAD_DIM, HEAD_DIM), HEAD_DIM)
                out_ref[rows, cols] = (att[rows, head_rows(h)] * column * gain_ref[:, cols]).astype(BF16)
        copies.append(pltpu.make_async_copy(out_ref.at[rows, :], out_hbm.at[rows, :], sems.at[step]))
        copies[-1].start()
    for copy in copies:
        copy.wait()


def local(queries, key_vectors, value_vectors, decay_rate, norm_gain, *, zp, nc, ne, nt):
    rows, width = queries.shape
    heads_all = width // HEAD_DIM
    blocks = rows // BLK
    group = zp * ne
    groups = nc // zp
    heads = heads_all // group
    part = heads * HEAD_DIM
    span = float(rows)
    vmem = pl.BlockSpec(memory_space=pltpu.VMEM)
    hbm = pl.BlockSpec(memory_space=pltpu.HBM)
    anywhere = pl.BlockSpec(memory_space=pl.ANY)
    ring = (0, 2, 1, 3) if group == 4 else tuple(range(group))
    ring3 = (0, 3, 2, 1) if group == 4 else tuple(range(group))
    state_type = jax.ShapeDtypeStruct((part, HEAD_DIM), F32)
    term_type = jax.ShapeDtypeStruct((max(blocks - 1, 1), part, HEAD_DIM), F32)
    held_type = jax.ShapeDtypeStruct((group, rows, part), BF16)
    where = dict(zp=zp, ne=ne)
    mirror = groups == 2 and zp == 2

    def call(kernel, count, outs, name, **more):
        more = {"in_specs": [vmem] * count, "out_specs": [vmem] * len(outs), "out_shape": outs, "name": name, **more}
        return pl.pallas_call(kernel, compiler_params=params(), **more)

    pinned = [pltpu.with_memory_space_constraint(a, pltpu.HBM) for a in (decay_rate, queries, key_vectors, value_vectors)]
    order = (3, 2, 1, 0) if group == 4 else ring[1:] + ring[:1]
    early = min(3, group)
    rates, query, key, value, *rest = call(
        functools.partial(load_kernel, heads=heads, blocks=blocks, order=order, mirror=mirror, early=early, **where),
        4,
        [jax.ShapeDtypeStruct((group, heads, 8, HEAD_DIM), F32), held_type, held_type, held_type]
        + [state_type] * early
        + [term_type] * early,
        "load",
        in_specs=[hbm] * 4,
        scratch_shapes=[pltpu.SMEM((heads_all,), F32), pltpu.SemaphoreType.DMA((4, group))],
    )(*pinned)

    slots, terms = dict(zip(order, rest[:early])), dict(zip(order, rest[early:]))
    for d in order[early:]:
        kernel = functools.partial(spread_kernel, d=d, blocks=blocks, heads=heads)
        slots[d], terms[d] = call(kernel, 3, [state_type, term_type], "spread")(rates, key, value)

    def swap(value, d):
        pairs = []
        for zz in range(nc):
            for xx in range(ne):
                m = ((zz % zp) * ne + xx) ^ d
                pairs.append((zz * ne + xx, (zz // zp * zp + m // ne) * ne + m % ne))
        return lax.ppermute(value, ("ctx", "exp"), pairs)

    slots = [slots[0]] + [swap(slots[d], d) for d in ring[1:]]

    local_part, inner = call(
        functools.partial(local_kernel, blocks=blocks, heads=heads, group=group),
        4,
        [jax.ShapeDtypeStruct((group, rows, part), F32), jax.ShapeDtypeStruct((group, heads, BLK, HEAD_DIM), F32)],
        "local_part",
        cost_estimate=pl.CostEstimate(flops=4 * rows * BLK * width, bytes_accessed=10 * rows * width, transcendentals=0),
    )(rates, query, key, value)

    (total,) = call(
        functools.partial(total_kernel, ring=ring, heads=heads, span=span, **where),
        group + 2,
        [state_type],
        "group_total",
        in_specs=[vmem, anywhere] + [vmem] * group,
    )(rates, inner, *slots)

    if groups == 2:
        before = lax.ppermute(total, "ctx", [(zz, nc - 1 - zz if mirror else (zz + zp) % nc) for zz in range(nc)])
    else:
        before = lax.ppermute(total, "ctx", [(zz, zz + zp) for zz in range(nc - zp)])
    step = 1
    while step < groups - 1:
        scale = jnp.exp(-rates[0, :, :1, :] * (span * group * step))
        moved = lax.ppermute(before, "ctx", [(zz, zz + zp * step) for zz in range(nc - zp * step)])
        before = before + (scale * moved.reshape(heads, HEAD_DIM, HEAD_DIM)).reshape(part, HEAD_DIM)
        step *= 2

    carries = call(
        functools.partial(carry_kernel, ring=ring, ring_out=ring3, heads=heads, span=span, **where), group + 2, [state_type] * group, "carry"
    )(rates, before, *slots)
    carries = [carries[0]] + [swap(carry, d) for carry, d in zip(carries[1:], ring3[1:])]

    attended, row_sum = [], None
    for i, d in enumerate(ring3):
        first, last = i == 0, i == group - 1
        att, row_sum = call(
            functools.partial(carried_kernel, d=d, blocks=blocks, heads=heads, first=first, last=last),
            6 if first else 7,
            [jax.ShapeDtypeStruct((rows, part), F32), jax.ShapeDtypeStruct((1, rows) if last else (rows, HEAD_DIM), F32)],
            "carried",
        )(rates, query, local_part, inner, terms[d], carries[i], *([] if first else [row_sum]))
        attended.append(att)

    if nt & (nt - 1) == 0:
        swaps = [[(i, i ^ d) for i in range(nt)] for d in range(1, nt)]
    else:
        swaps = [[(i, (i + d) % nt) for i in range(nt)] for d in range(1, nt)]
    row_sums = [row_sum] + [lax.ppermute(row_sum, "tp", pairs) for pairs in swaps]

    steps = 4
    norm = functools.partial(norm_kernel, features=float(width * nt), count=nt, steps=steps, ring=ring3, heads=heads, mirror=mirror, **where)
    (out,) = call(
        norm,
        nt + 1 + group,
        [jax.ShapeDtypeStruct((rows, width), BF16)],
        "norm",
        out_specs=[hbm],
        scratch_shapes=[
            pltpu.VMEM((rows, width), BF16),
            pltpu.SemaphoreType.DMA((steps,)),
        ],
    )(*row_sums, norm_gain[None, :], *attended)
    return out


def solution(mesh):
    nc, ne, nt = mesh.shape["ctx"], mesh.shape["exp"], mesh.shape["tp"]

    def whole(queries, key_vectors, value_vectors, decay_rate, norm_gain):
        heads_local = decay_rate.shape[0] // nt
        zp = 2 if nc % 2 == 0 and heads_local % (2 * ne) == 0 else 1
        return jax.shard_map(
            functools.partial(local, zp=zp, nc=nc, ne=ne, nt=nt),
            mesh=mesh,
            in_specs=(P(("ctx", "exp"), "tp"),) * 3 + (P("tp"), P("tp")),
            out_specs=P(("ctx", "exp"), "tp"),
            check_vma=False,
        )(queries, key_vectors, value_vectors, decay_rate, norm_gain)

    return whole
```

```python
import functools
import jax
import jax.numpy as jnp
from jax import lax
from jax.experimental import pallas as pl
from jax.experimental.pallas import tpu as pltpu
from jax.sharding import PartitionSpec as P

HEAD_DIM = 128
BLK = 256
F32 = jnp.float32
BF16 = jnp.bfloat16


def dot(a, b, dims):
    return lax.dot_general(a, b, (dims, ((), ())), preferred_element_type=F32)


def params(mib=32):
    return pltpu.CompilerParams(vmem_limit_bytes=mib << 20)


def head_rows(h):
    return slice(h * HEAD_DIM, (h + 1) * HEAD_DIM)


def member(zp, ne):
    return (lax.axis_index("ctx") % zp) * ne + lax.axis_index("exp")


def away(way):
    even, odd = way
    return even if even == odd else jnp.where(lax.axis_index("tp") % 2 == 0, even, odd)


def owned(zp, ne, mirror):
    me = member(zp, ne)
    return me ^ (lax.axis_index("ctx") // zp % 2 * ne) if mirror else me


def spread(d, rate_of, key_ref, value_ref, state_ref, terms_ref, blocks, heads):
    left = (BLK - lax.broadcasted_iota(jnp.int32, (BLK, HEAD_DIM), 0)).astype(F32)
    for h in range(heads):
        here = head_rows(h)
        rate = rate_of(h)
        tail = jnp.exp(-rate * left)
        block_decay = jnp.exp(-rate * BLK)
        own = None
        for b in range(blocks):
            rows = slice(b * BLK, (b + 1) * BLK)
            keys = (key_ref[d, rows, here].astype(F32) * tail).astype(BF16)
            term = dot(keys, value_ref[d, rows, here], ((0,), (0,)))
            if b < blocks - 1:
                terms_ref[b, here, :] = term
            own = term if own is None else block_decay * own + term
        state_ref[here, :] = own


def load_kernel(rate_hbm, query_hbm, key_hbm, value_hbm, *refs, zp, ne, mirror, heads, blocks, order, early, ways):
    rates_ref, query_ref, key_ref, value_ref = refs[:4]
    states, terms, (rate_smem, sems) = refs[4 : 4 + early], refs[4 + early : 4 + 2 * early], refs[4 + 2 * early :]
    me = owned(zp, ne, mirror)
    part = heads * HEAD_DIM

    def copy_of(n, d):
        source, held = ((key_hbm, key_ref), (value_hbm, value_ref), (query_hbm, query_ref))[n]
        cols = pl.ds(pl.multiple_of((me ^ away(ways[d])) * part, part), part)
        return pltpu.make_async_copy(source.at[:, cols], held.at[d], sems.at[n, d])

    rate_copy = pltpu.make_async_copy(rate_hbm, rate_smem, sems.at[3, 0])
    rate_copy.start()
    for d in order:
        copy_of(0, d).start()
        copy_of(1, d).start()
    for d in order:
        copy_of(2, d).start()
    rate_copy.wait()
    for d in order:
        for h in range(heads):
            rates_ref[d, h] = jnp.full((8, HEAD_DIM), rate_smem[(me ^ away(ways[d])) * heads + h], F32)
    for i, d in enumerate(order):
        copy_of(0, d).wait()
        copy_of(1, d).wait()
        if i < early:
            spread(d, lambda h: rates_ref[d, h][:1, :], key_ref, value_ref, states[i], terms[i], blocks, heads)
    for d in order:
        copy_of(2, d).wait()


def spread_kernel(rates_ref, key_ref, value_ref, state_ref, terms_ref, *, d, blocks, heads):
    spread(d, lambda h: rates_ref[d, h][:1, :], key_ref, value_ref, state_ref, terms_ref, blocks, heads)


def local_kernel(rates_ref, query_ref, key_ref, value_ref, out_ref, inner_ref, *, blocks, heads, group):
    sub = HEAD_DIM
    count = BLK // sub
    i = lax.broadcasted_iota(jnp.int32, (sub, sub), 0)
    j = lax.broadcasted_iota(jnp.int32, (sub, sub), 1)
    apart = (i - j).astype(F32)
    offset = lax.broadcasted_iota(jnp.int32, (BLK, HEAD_DIM), 0).astype(F32)
    for d in range(group):
        for h in range(heads):
            rate = rates_ref[d, h][:1, :]
            weights = [jnp.where(apart >= 0, jnp.exp(-rate * jnp.maximum(apart, 0.0)), 0.0)]
            weights += [jnp.exp(-rate * (apart + float(sub * n))) for n in range(1, count)]
            inner_ref[d, h] = jnp.exp(-rate * offset)
            cols = head_rows(h)
            for b in range(blocks):
                for n in range(count):
                    rows = slice(b * BLK + n * sub, b * BLK + (n + 1) * sub)
                    seen = slice(b * BLK, b * BLK + (n + 1) * sub)
                    scores = dot(query_ref[d, rows, cols], key_ref[d, seen, cols], ((1,), (1,)))
                    weight = weights[0] if n == 0 else jnp.concatenate(weights[n::-1], axis=1)
                    mixing = (scores * weight).astype(BF16)
                    out_ref[d, rows, cols] = dot(mixing, value_ref[d, seen, cols], ((1,), (0,)))


def span_weight(rate, gap, span):
    return jnp.where(gap >= 0, jnp.exp(-rate * (jnp.maximum(gap, 0).astype(F32) * span)), 0.0)


def total_kernel(rates_ref, after_ref, *refs, ring, heads, span, zp, ne, ways):
    group = len(ring)
    slots, out = refs[:group], refs[group]
    me = member(zp, ne)
    for h in range(heads):
        rate = rates_ref[0, h][:1, :]
        total = None
        for e, slot in zip(ring, slots):
            part = span_weight(rate, group - 1 - (me ^ away(ways[e])), span) * slot[head_rows(h), :]
            total = part if total is None else total + part
        out[head_rows(h), :] = total


def carry_kernel(rates_ref, before_ref, *refs, ring, ring_out, heads, span, zp, ne, ways):
    group = len(ring)
    slots, outs = refs[:group], refs[group:]
    me = member(zp, ne)
    has_before = lax.axis_index("ctx") >= zp
    for h in range(heads):
        rate = rates_ref[0, h][:1, :]
        parts = [slot[head_rows(h), :] for slot in slots]
        before = jnp.where(has_before, before_ref[head_rows(h), :], 0.0)
        for d, out in zip(ring_out, outs):
            at = me ^ away(ways[d])
            carry = span_weight(rate, at, span) * before
            for e, part in zip(ring, parts):
                if e != d:
                    carry = carry + span_weight(rate, at - (me ^ away(ways[e])) - 1, span) * part
            out[head_rows(h), :] = carry


def carried_kernel(rates_ref, query_ref, local_ref, inner_ref, terms_ref, carry_ref, *refs, d, blocks, heads, first, last):
    earlier_ref = None if first else refs[0]
    att_ref, acc_ref = refs[0 if first else 1 :][:2]
    sums = []
    for h in range(heads):
        here = head_rows(h)
        block_decay = jnp.exp(-rates_ref[d, h][:1, :] * BLK)
        state = carry_ref[here, :]
        for b in range(blocks):
            rows = slice(b * BLK, (b + 1) * BLK)
            carried = dot(query_ref[d, rows, here], state.astype(BF16), ((1,), (0,)))
            att = local_ref[d, rows, here] + carried * inner_ref[d, h]
            att_ref[rows, here] = att
            square = att * att
            if h > 0:
                square = square + sums[b]
                sums[b] = square
            else:
                sums.append(square)
            if b < blocks - 1:
                state = block_decay * state + terms_ref[b, here, :]
    for b in range(blocks):
        rows = slice(b * BLK, (b + 1) * BLK)
        square = sums[b] if first else sums[b] + earlier_ref[rows, :]
        if last:
            for at in range(0, BLK, HEAD_DIM):
                turned = jnp.transpose(square[at : at + HEAD_DIM, :])
                acc_ref[:, b * BLK + at : b * BLK + at + HEAD_DIM] = jnp.sum(turned, axis=0, keepdims=True)
        else:
            acc_ref[rows, :] = square


def norm_kernel(*refs, features, count, steps, ring, zp, ne, mirror, heads, ways):
    squares, gain_ref, refs = refs[:count], refs[count], refs[count + 1 :]
    atts, (out_hbm, out_ref, sems) = refs[: len(ring)], refs[len(ring) :]
    me = owned(zp, ne, mirror)
    total = squares[0][...]
    for other in squares[1:]:
        total = total + other[...]
    inverse = lax.rsqrt(total / features + 1e-06)
    height = out_ref.shape[0] // steps
    copies = []
    for step in range(steps):
        rows = slice(step * height, (step + 1) * height)
        tiles = [inverse[:, at : at + HEAD_DIM] for at in range(step * height, (step + 1) * height, HEAD_DIM)]
        column = jnp.concatenate([jnp.transpose(jnp.broadcast_to(tile, (HEAD_DIM, HEAD_DIM))) for tile in tiles], axis=0)
        for att, d in zip(atts, ring):
            for h in range(heads):
                cols = pl.ds(pl.multiple_of(((me ^ away(ways[d])) * heads + h) * HEAD_DIM, HEAD_DIM), HEAD_DIM)
                out_ref[rows, cols] = (att[rows, head_rows(h)] * column * gain_ref[:, cols]).astype(BF16)
        copies.append(pltpu.make_async_copy(out_ref.at[rows, :], out_hbm.at[rows, :], sems.at[step]))
        copies[-1].start()
    for copy in copies:
        copy.wait()


def local(queries, key_vectors, value_vectors, decay_rate, norm_gain, *, zp, nc, ne, nt):
    rows, width = queries.shape
    heads_all = width // HEAD_DIM
    blocks = rows // BLK
    group = zp * ne
    groups = nc // zp
    heads = heads_all // group
    part = heads * HEAD_DIM
    span = float(rows)
    vmem = pl.BlockSpec(memory_space=pltpu.VMEM)
    hbm = pl.BlockSpec(memory_space=pltpu.HBM)
    anywhere = pl.BlockSpec(memory_space=pl.ANY)
    if group == 4:
        ways, ring, ring3, order = ((0, 0), (1, 3), (2, 1), (3, 2)), (0, 1, 2, 3), (0, 1, 3, 2), (3, 2, 1, 0)
    else:
        ways, ring = tuple((d, d) for d in range(group)), tuple(range(group))
        ring3, order = ring, ring[1:] + ring[:1]
    state_type = jax.ShapeDtypeStruct((part, HEAD_DIM), F32)
    term_type = jax.ShapeDtypeStruct((max(blocks - 1, 1), part, HEAD_DIM), F32)
    held_type = jax.ShapeDtypeStruct((group, rows, part), BF16)
    where = dict(zp=zp, ne=ne)
    mirror = groups == 2 and zp == 2

    def call(kernel, count, outs, name, **more):
        more = {"in_specs": [vmem] * count, "out_specs": [vmem] * len(outs), "out_shape": outs, "name": name, **more}
        return pl.pallas_call(kernel, compiler_params=params(), **more)

    pinned = [pltpu.with_memory_space_constraint(a, pltpu.HBM) for a in (decay_rate, queries, key_vectors, value_vectors)]
    early = min(3, group)
    rates, query, key, value, *rest = call(
        functools.partial(load_kernel, heads=heads, blocks=blocks, order=order, mirror=mirror, early=early, ways=ways, **where),
        4,
        [jax.ShapeDtypeStruct((group, heads, 8, HEAD_DIM), F32), held_type, held_type, held_type]
        + [state_type] * early
        + [term_type] * early,
        "load",
        in_specs=[hbm] * 4,
        scratch_shapes=[pltpu.SMEM((heads_all,), F32), pltpu.SemaphoreType.DMA((4, group))],
    )(*pinned)

    slots, terms = dict(zip(order, rest[:early])), dict(zip(order, rest[early:]))
    for d in order[early:]:
        kernel = functools.partial(spread_kernel, d=d, blocks=blocks, heads=heads)
        slots[d], terms[d] = call(kernel, 3, [state_type, term_type], "spread")(rates, key, value)

    def swap(value, d):
        pairs = []
        for zz in range(nc):
            for xx in range(ne):
                for tt in range(nt):
                    m = ((zz % zp) * ne + xx) ^ ways[d][tt % 2]
                    to = (zz // zp * zp + m // ne) * ne + m % ne
                    pairs.append(((zz * ne + xx) * nt + tt, to * nt + tt))
        return lax.ppermute(value, ("ctx", "exp", "tp"), pairs)

    slots = [slots[0]] + [swap(slots[d], d) for d in ring[1:]]

    local_part, inner = call(
        functools.partial(local_kernel, blocks=blocks, heads=heads, group=group),
        4,
        [jax.ShapeDtypeStruct((group, rows, part), F32), jax.ShapeDtypeStruct((group, heads, BLK, HEAD_DIM), F32)],
        "local_part",
        cost_estimate=pl.CostEstimate(flops=4 * rows * BLK * width, bytes_accessed=10 * rows * width, transcendentals=0),
    )(rates, query, key, value)

    (total,) = call(
        functools.partial(total_kernel, ring=ring, ways=ways, heads=heads, span=span, **where),
        group + 2,
        [state_type],
        "group_total",
        in_specs=[vmem, anywhere] + [vmem] * group,
    )(rates, inner, *slots)

    if groups == 2:
        before = lax.ppermute(total, "ctx", [(zz, nc - 1 - zz if mirror else (zz + zp) % nc) for zz in range(nc)])
    else:
        before = lax.ppermute(total, "ctx", [(zz, zz + zp) for zz in range(nc - zp)])
    step = 1
    while step < groups - 1:
        scale = jnp.exp(-rates[0, :, :1, :] * (span * group * step))
        moved = lax.ppermute(before, "ctx", [(zz, zz + zp * step) for zz in range(nc - zp * step)])
        before = before + (scale * moved.reshape(heads, HEAD_DIM, HEAD_DIM)).reshape(part, HEAD_DIM)
        step *= 2

    carries = call(
        functools.partial(carry_kernel, ring=ring, ways=ways, ring_out=ring3, heads=heads, span=span, **where), group + 2, [state_type] * group, "carry"
    )(rates, before, *slots)
    carries = [carries[0]] + [swap(carry, d) for carry, d in zip(carries[1:], ring3[1:])]

    attended, row_sum = [], None
    for i, d in enumerate(ring3):
        first, last = i == 0, i == group - 1
        att, row_sum = call(
            functools.partial(carried_kernel, d=d, blocks=blocks, heads=heads, first=first, last=last),
            6 if first else 7,
            [jax.ShapeDtypeStruct((rows, part), F32), jax.ShapeDtypeStruct((1, rows) if last else (rows, HEAD_DIM), F32)],
            "carried",
        )(rates, query, local_part, inner, terms[d], carries[i], *([] if first else [row_sum]))
        attended.append(att)

    if nt & (nt - 1) == 0:
        swaps = [[(i, i ^ d) for i in range(nt)] for d in range(1, nt)]
    else:
        swaps = [[(i, (i + d) % nt) for i in range(nt)] for d in range(1, nt)]
    row_sums = [row_sum] + [lax.ppermute(row_sum, "tp", pairs) for pairs in swaps]

    steps = 4
    norm = functools.partial(norm_kernel, features=float(width * nt), count=nt, steps=steps, ring=ring3, heads=heads, mirror=mirror, ways=ways, **where)
    (out,) = call(
        norm,
        nt + 1 + group,
        [jax.ShapeDtypeStruct((rows, width), BF16)],
        "norm",
        out_specs=[hbm],
        scratch_shapes=[
            pltpu.VMEM((rows, width), BF16),
            pltpu.SemaphoreType.DMA((steps,)),
        ],
    )(*row_sums, norm_gain[None, :], *attended)
    return out


def solution(mesh):
    nc, ne, nt = mesh.shape["ctx"], mesh.shape["exp"], mesh.shape["tp"]

    def whole(queries, key_vectors, value_vectors, decay_rate, norm_gain):
        heads_local = decay_rate.shape[0] // nt
        zp = 2 if nc % 2 == 0 and heads_local % (2 * ne) == 0 else 1
        return jax.shard_map(
            functools.partial(local, zp=zp, nc=nc, ne=ne, nt=nt),
            mesh=mesh,
            in_specs=(P(("ctx", "exp"), "tp"),) * 3 + (P("tp"), P("tp")),
            out_specs=P(("ctx", "exp"), "tp"),
            check_vma=False,
        )(queries, key_vectors, value_vectors, decay_rate, norm_gain)

    return whole
```
